32 devices in a mesh: grp: 2 (over y), seq: 4 (over z), head: 2 (over x), rep: 2 (over core).
Axes of the slice: x: 2, y: 2, z: 4, core: 2. Of those that a mesh axis runs over, the one named last changes fastest.
Arguments:
- query_latent: bfloat16 [1024, 32, 512], P(('grp', 'seq'), ('head', 'rep')), parts along dimension 0, may hold values from -400 to 400
- query_rope: bfloat16 [1024, 2048], P(('grp', 'seq'), ('head', 'rep')), parts along dimension 0, may hold values from -4 to 4
- latent: bfloat16 [8192, 512], P(('grp', 'seq', 'rep')), parts along dimension 0, may hold values from -6 to 6
- key_rope: bfloat16 [64, 8192], P(None, ('grp', 'seq', 'rep')), parts along dimension 1, may hold values from -4 to 4
- value_up: bfloat16 [32, 512, 128], P(('head', 'rep')), may hold values from -2.390625 to 2.390625
- out_proj: bfloat16 [4096, 3584], P(('head', 'rep')), may hold values from -0.09375 to 0.09375
Outputs:
- output: bfloat16 [1024, 3584], P(('grp', 'seq', 'head', 'rep')), parts along dimension 0
The draws below stay inside these ranges and needn't reach their ends.
There are 2 independent parts, one for each index of `grp`. The reference program is written for one: setup_inputs(seed, part) draws one part's arguments, and reference() takes and returns one part's arrays. A program takes and returns all parts, laid end to end along the dimension named above; an argument that names none is the same for every part. Nothing has to cross between parts.
All inputs are finite; a program needn't handle non-finite values.
Results may differ from the reference program's by a relative error of at most 0.017.
Values may be sent and summed in bfloat16 or wider, within the bound.
A program may use at most 128 MiB of HBM per device.

```python
import jax
import jax.numpy as jnp
from jax import lax

H = 32
D = 3584
DL = 512
DR = 64
VD = 128
Q_DEV = 128
KB = 1024
TOKENS = 4096
QTOK = 512
N_SEQ = 4


def joint_draw(key):
    lat_key = jax.random.fold_in(key, 7001)
    query_key = jax.random.fold_in(key, 7002)
    tokens = KB * N_SEQ
    queries = Q_DEV * N_SEQ
    latents = jnp.clip(jax.random.normal(lat_key, (tokens, DL), jnp.float32), -4.0, 4.0)
    query_values = jnp.clip(jax.random.normal(query_key, (queries, H, DL), jnp.float32), -4.0, 4.0)
    return (latents, query_values)


def draw_query_latent(key, part):
    latents, query_values = joint_draw(key)
    return query_values.astype(jnp.bfloat16)


def draw_latent(key, part):
    latents, query_values = joint_draw(key)
    return latents.astype(jnp.bfloat16)


def steps_of(key, shape, split, smallest, largest):
    level = 1.0
    for dim, shards_of in split:
        heights = jax.random.uniform(jax.random.fold_in(jax.random.fold_in(key, 6), dim), (shards_of,), jnp.float32, smallest / len(split), largest / len(split))
        level = level * jnp.repeat(jnp.exp(heights), shape[dim] // shards_of).reshape((-1,) + (1,) * (len(shape) - 1 - dim))
    return level


def normal_values(stream_key, dims, deviation, limit, cuts=(), kind=jnp.bfloat16):
    array = deviation * jax.random.normal(stream_key, dims, jnp.float32)
    if cuts:
        array = array * steps_of(stream_key, dims, cuts, -0.22, 0.18)
    return jnp.clip(array, -limit, limit).astype(kind)


def setup_inputs(seed: int = 0, part: int = 0) -> dict:
    arg_keys = jax.random.split(jax.random.key(seed), 7)
    part_keys = jax.random.split(jax.random.fold_in(arg_keys[6], part), 7)
    return {
        "query_latent": draw_query_latent(jax.random.fold_in(jax.random.fold_in(arg_keys[6], part), 71), part),
        "query_rope": normal_values(part_keys[1], (QTOK, H * DR), 1.0, 4.0, ((0, 4), (1, 4))),
        "latent": draw_latent(jax.random.fold_in(jax.random.fold_in(arg_keys[6], part), 71), part),
        "key_rope": normal_values(part_keys[3], (DR, TOKENS), 1.0, 4.0, ((1, 8),)),
        "value_up": normal_values(arg_keys[4], (H, DL, VD), 0.4, 2.390625, ((0, 4),)),
        "out_proj": normal_values(arg_keys[5], (H * VD, D), (H * VD) ** -0.5, 0.09375, ((0, 4),)),
    }


def reference(query_latent, query_rope, latent, key_rope, value_up, out_proj):
    levels = min(4, N_SEQ // 4 + 1)
    score_scale = (DL + DR) ** -0.5
    query_index = jnp.arange(Q_DEV, dtype=jnp.int32)
    key_index = jnp.arange(KB, dtype=jnp.int32)

    def one_shard(shard_index):
        queries = lax.dynamic_slice_in_dim(query_latent, (shard_index * Q_DEV).astype(jnp.int32), Q_DEV, 0).astype(jnp.float32)
        rope_queries = lax.dynamic_slice_in_dim(query_rope, (shard_index * Q_DEV).astype(jnp.int32), Q_DEV, 0)
        rope_queries = rope_queries.reshape(Q_DEV, H, DR).astype(jnp.float32)
        latents = [lax.dynamic_slice_in_dim(latent, (shard_index * KB).astype(jnp.int32), KB, 0)]
        rope_blocks = [lax.dynamic_slice_in_dim(key_rope, (shard_index * KB).astype(jnp.int32), KB, 1)]
        allowed = [key_index[None, :] <= (KB - Q_DEV + query_index)[:, None]]
        for level_index in range(levels):
            source = shard_index - 2 ** level_index
            block_start = (jnp.maximum(source, 0) * KB).astype(jnp.int32)
            latents.append(lax.dynamic_slice_in_dim(latent, block_start, KB, 0))
            rope_blocks.append(lax.dynamic_slice_in_dim(key_rope, block_start, KB, 1))
            allowed.append(jnp.broadcast_to(source >= 0, (Q_DEV, KB)))
        key_latent = jnp.concatenate(latents, axis=0).astype(jnp.float32)
        key_ropes = jnp.concatenate(rope_blocks, axis=1).astype(jnp.float32)
        visible = jnp.concatenate(allowed, axis=1)
        scores = jnp.einsum("qhc,kc->hqk", queries, key_latent, precision=lax.Precision.HIGHEST)
        scores = scores + jnp.einsum("qhr,rk->hqk", rope_queries, key_ropes, precision=lax.Precision.HIGHEST)
        scores = jnp.where(visible[None], scores * score_scale, -1.0e30)
        row_max = jnp.max(scores, axis=2, keepdims=True)
        weights = jnp.exp(scores - row_max)
        row_total = jnp.sum(weights, axis=2, keepdims=True)
        rounded = lax.optimization_barrier(weights.astype(jnp.bfloat16)).astype(jnp.float32)
        attended = jnp.einsum("hqk,kc->hqc", rounded, key_latent, precision=lax.Precision.HIGHEST) / row_total
        attended = attended.astype(jnp.bfloat16).astype(jnp.float32)
        expanded = jnp.einsum("hqc,hcv->qhv", attended, value_up.astype(jnp.float32), precision=lax.Precision.HIGHEST)
        expanded = expanded.astype(jnp.bfloat16).reshape(Q_DEV, H * VD)
        return jnp.dot(expanded, out_proj, preferred_element_type=jnp.float32).astype(jnp.bfloat16)

    output = lax.map(one_shard, jnp.arange(N_SEQ, dtype=jnp.int32))
    return output.reshape(N_SEQ * Q_DEV, D)
```

```python
import functools
import math

import jax
import jax.numpy as jnp
from jax import lax
from jax.experimental import pallas as pl
from jax.experimental.pallas import tpu as pltpu
from jax.sharding import PartitionSpec as P

lanes = 128
masked_score = -1e30
MESH = pl.DeviceIdType.MESH


def tile_rows(rows, most):
    tile = min(rows, most)
    while rows % tile:
        tile -= 8
    return tile


def column_width(columns, most):
    width = most
    while columns % width:
        width -= lanes
    return width


def kernel(
    dims,
    query_hbm,
    query_rope_hbm,
    latent_hbm,
    rope_hbm,
    value_up_hbm,
    out_proj_hbm,
    out_ref,
    keys,
    query_in,
    query_rope_in,
    rope_in,
    value_up,
    out_proj,
    queries,
    rope_wide,
    rope_queries,
    row_max,
    row_sum,
    attended,
    expanded,
    partial,
    core_out,
    core_in,
    head_out,
    head_in,
    local_sem,
    own_send,
    own_recv,
    seq_send,
    seq_recv,
    head_send,
    head_recv,
    core_send,
    core_recv,
    sum_core_send,
    sum_core_recv,
    sum_head_send,
    sum_head_recv,
):
    n_seq, n_head, levels, heads, q_dev, width, rope_width, chunk, per_share = dims
    rows = q_dev * heads
    half = latent_hbm.shape[0]
    chunks = half // chunk
    pack = keys.shape[3] - chunk
    z = lax.axis_index("seq")
    x = lax.axis_index("head")
    c = lax.axis_index("rep")
    sibling = 1 - c
    scale = (width + rope_width) ** (-0.5) * math.log2(math.e)

    latent_loads = [
        pltpu.make_async_copy(
            latent_hbm.at[pl.ds(j * chunk, chunk), :],
            keys.at[0, c, j, pl.ds(0, chunk), :],
            local_sem.at[j],
        )
        for j in range(chunks)
    ]
    rope_load = pltpu.make_async_copy(rope_hbm, rope_in, local_sem.at[chunks])
    query_load = pltpu.make_async_copy(query_hbm, query_in, local_sem.at[chunks + 1])
    query_rope_load = pltpu.make_async_copy(
        query_rope_hbm, query_rope_in, local_sem.at[chunks + 2]
    )
    value_load = pltpu.make_async_copy(value_up_hbm, value_up, local_sem.at[chunks + 3])
    proj_load = pltpu.make_async_copy(out_proj_hbm, out_proj, local_sem.at[chunks + 4])
    rope_load.start()
    for load in latent_loads:
        load.start()
    query_load.start()
    query_rope_load.start()

    hops = sorted({1} | {2 ** (b - 1) for b in range(1, levels)})
    barrier = pltpu.get_barrier_semaphore()
    pl.semaphore_signal(barrier, inc=1, device_id={"rep": sibling}, device_id_type=MESH)
    for k in range(1, n_head):
        pl.semaphore_signal(
            barrier, inc=1, device_id={"head": lax.rem(x + k, n_head)}, device_id_type=MESH
        )
    for hop in hops:

        @pl.when(z >= hop)
        def _():
            pl.semaphore_signal(
                barrier, inc=1, device_id={"seq": z - hop}, device_id_type=MESH
            )

    rope_load.wait()
    for load in latent_loads:
        load.wait()
    value_load.start()
    proj_load.start()
    per_row = width // chunk
    for j in range(chunks):
        for k in range(per_row):
            keys[0, c, j, chunk : chunk + pack, k * chunk : (k + 1) * chunk] = rope_in[
                k * pack : (k + 1) * pack, j * chunk : (j + 1) * chunk
            ]

    targets = n_head
    for hop in hops:
        targets = targets + jnp.where(z + hop < n_seq, 1, 0)
    pl.semaphore_wait(barrier, targets)

    def share(k):
        return lax.rem(x + n_head - k, n_head)

    def place(b, r, k, i):
        return keys.at[b, r, share(k) * per_share + i]

    def seq_copy(b, i):
        hop = 1 if b == 1 else 2 ** (b - 2)
        return pltpu.make_async_remote_copy(
            src_ref=place(b - 1, c, 0, i),
            dst_ref=place(b, c, 0, i),
            send_sem=seq_send.at[b - 1, i],
            recv_sem=seq_recv.at[b - 1, i],
            device_id={"seq": jnp.minimum(z + hop, n_seq - 1)},
            device_id_type=MESH,
        )

    def seq_start(b, i):
        hop = 1 if b == 1 else 2 ** (b - 2)
        return (z + hop < n_seq) & (z >= (0 if b == 1 else 2 ** (b - 2)))

    def head_copy(b, k, i):
        return pltpu.make_async_remote_copy(
            src_ref=place(b, c, 0, i),
            dst_ref=place(b, c, 0, i),
            send_sem=head_send.at[b - 1, k - 1, i],
            recv_sem=head_recv.at[b - 1, k - 1, i],
            device_id={"head": lax.rem(x + k, n_head)},
            device_id_type=MESH,
        )

    def head_arrival(b, k, i):
        return pltpu.make_async_remote_copy(
            src_ref=place(b, c, k, i),
            dst_ref=place(b, c, k, i),
            send_sem=head_send.at[b - 1, k - 1, i],
            recv_sem=head_recv.at[b - 1, k - 1, i],
            device_id={"head": lax.rem(x + k, n_head)},
            device_id_type=MESH,
        )

    def core_copy(b, k, i, r):
        return pltpu.make_async_remote_copy(
            src_ref=place(b, r, k, i),
            dst_ref=place(b, r, k, i),
            send_sem=core_send.at[b - 1, k, i],
            recv_sem=core_recv.at[b - 1, k, i],
            device_id={"rep": sibling},
            device_id_type=MESH,
        )

    def own_copy(r):
        return pltpu.make_async_remote_copy(
            src_ref=keys.at[0, r],
            dst_ref=keys.at[0, r],
            send_sem=own_send,
            recv_sem=own_recv,
            device_id={"rep": sibling},
            device_id_type=MESH,
        )

    def send_on(b, i):
        @pl.when(z >= 2 ** (b - 1))
        def _():
            seq_copy(b, i).wait_recv()
            if b < levels:

                @pl.when(seq_start(b + 1, i))
                def _():
                    seq_copy(b + 1, i).start()

            for k in range(1, n_head):
                head_copy(b, k, i).start()
            core_copy(b, 0, i, c).start()

    def pass_core(b, k, i):
        @pl.when(z >= 2 ** (b - 1))
        def _():
            head_arrival(b, k, i).wait_recv()
            core_copy(b, k, i, c).start()

    for i in range(per_share):

        @pl.when(seq_start(1, i))
        def _():
            seq_copy(1, i).start()

    own_copy(c).start()

    query_load.wait()
    query_rope_load.wait()
    if len(query_in.shape) == 3:
        step_q = q_dev // 4
        for part in range(4):
            queries[part * step_q * heads : (part + 1) * step_q * heads, :] = (
                query_in[part * step_q : (part + 1) * step_q]
                .astype(jnp.float32)
                .reshape(step_q * heads, width)
                .astype(jnp.bfloat16)
            )
        query_source = queries
    else:
        query_source = query_in
    for h in range(heads):
        start = h * rope_width // lanes * lanes
        shift = h * rope_width - start
        piece = query_rope_in[:, start : start + lanes].astype(jnp.float32)
        if shift:
            piece = pltpu.roll(piece, lanes - shift, 1)
        rope_wide[pl.ds(h, q_dev, stride=heads), :] = piece
    rope_queries[...] = rope_wide[:, :rope_width].astype(jnp.bfloat16)

    tile = tile_rows(rows, 256)

    def attend(places, first=False, key_base=None):
        def key_rows():
            return jnp.concatenate([keys[b, r, j, :chunk, :] for b, r, j in places], axis=0)

        def key_ropes():
            return jnp.concatenate(
                [
                    jnp.concatenate(
                        [
                            keys[b, r, j, chunk : chunk + pack, k * chunk : (k + 1) * chunk]
                            for k in range(per_row)
                        ],
                        axis=0,
                    )
                    for b, r, j in places
                ],
                axis=1,
            )

        def scores_of(base):
            at = pl.ds(base, tile)
            scores = lax.dot_general(
                query_source[at, :],
                key_rows(),
                (((1,), (1,)), ((), ())),
                preferred_element_type=jnp.float32,
            )
            scores = scores + jnp.dot(
                rope_queries[at, :], key_ropes(), preferred_element_type=jnp.float32
            )
            if key_base is not None:
                key = key_base + lax.broadcasted_iota(jnp.int32, scores.shape, 1)
                row = base + lax.broadcasted_iota(jnp.int32, scores.shape, 0)
                limit = (2 * half - q_dev) + row // heads
                scores = jnp.where(key <= limit, scores, masked_score)
            return scores * scale

        def fold(base, scores):
            at = pl.ds(base, tile)
            top = jnp.max(scores, axis=1, keepdims=True)
            if not first:
                old = row_max[at, :1]
                top = jnp.maximum(top, old)
            weights = jnp.exp2(scores - top)
            part = weights[:, :lanes]
            for k in range(1, weights.shape[1] // lanes):
                part = part + weights[:, k * lanes : (k + 1) * lanes]
            update = jnp.dot(
                weights.astype(jnp.bfloat16), key_rows(), preferred_element_type=jnp.float32
            )
            if first:
                row_sum[at, :] = part
            else:
                factor = jnp.exp2(old - top)
                row_sum[at, :] = row_sum[at, :] * factor + part
            for k in range(width // lanes):
                piece = update[:, k * lanes : (k + 1) * lanes]
                if not first:
                    piece = attended[k, at, :] * factor + piece
                attended[k, at, :] = piece
            row_max[at, :] = jnp.broadcast_to(top, (tile, lanes))

        def body(step, _):
            base = pl.multiple_of(step * (2 * tile), tile)
            left = scores_of(base)
            right = scores_of(base + tile)
            fold(base, left)
            fold(base + tile, right)
            return 0

        lax.fori_loop(0, rows // (2 * tile), body, 0)

    def attend_share(b, k):
        @pl.when(z >= 2 ** (b - 1))
        def _():
            for i in range(per_share):
                core_copy(b, k, i, sibling).wait_recv()
            attend(
                [
                    (b, r, share(k) * per_share + i)
                    for r in (c, sibling)
                    for i in range(per_share)
                ]
            )

    attend([(0, c, j) for j in range(chunks)], first=True, key_base=c * half)
    send_on(1, 0)
    own_copy(sibling).wait_recv()
    attend([(0, sibling, j) for j in range(chunks)], key_base=sibling * half)
    for i in range(1, per_share):
        send_on(1, i)
    for b in range(1, levels + 1):
        for k in range(1, n_head):
            pass_core(b, k, 0)
        attend_share(b, 0)
        if b < levels:
            send_on(b + 1, 0)
        for k in range(1, n_head):
            for i in range(1, per_share):
                pass_core(b, k, i)
        for k in range(1, n_head):
            attend_share(b, k)
        if b < levels:
            for i in range(1, per_share):
                send_on(b + 1, i)

    value_load.wait()

    def normalise(step, _):
        at = pl.ds(pl.multiple_of(step * tile, tile), tile)
        inverse = 1.0 / jnp.sum(row_sum[at, :], axis=1, keepdims=True)
        for k in range(width // lanes):
            attended[k, at, :] = attended[k, at, :] * inverse
        return 0

    lax.fori_loop(0, rows // tile, normalise, 0)
    value_width = value_up.shape[2]
    for h in range(heads):
        latent_out = jnp.concatenate(
            [
                attended[k, pl.ds(h, q_dev, stride=heads), :].astype(jnp.bfloat16)
                for k in range(width // lanes)
            ],
            axis=1,
        )
        expanded[:, h * value_width : (h + 1) * value_width] = jnp.dot(
            latent_out, value_up[h], preferred_element_type=jnp.float32
        ).astype(jnp.bfloat16)

    proj_load.wait()
    columns, out_rows = core_out.shape[3], core_out.shape[2]
    pieces = core_out.shape[0]

    def sum_core(piece):
        return pltpu.make_async_remote_copy(
            src_ref=core_out.at[piece],
            dst_ref=core_in.at[piece],
            send_sem=sum_core_send.at[piece],
            recv_sem=sum_core_recv.at[piece],
            device_id={"rep": sibling},
            device_id_type=MESH,
        )

    def sum_head(piece, k):
        return pltpu.make_async_remote_copy(
            src_ref=head_out.at[piece, k - 1],
            dst_ref=head_in.at[piece, k - 1],
            send_sem=sum_head_send.at[piece, k - 1],
            recv_sem=sum_head_recv.at[piece, k - 1],
            device_id={"head": lax.rem(x + k, n_head)},
            device_id_type=MESH,
        )

    def project(piece):
        product = jnp.dot(
            expanded[...],
            out_proj[:, piece * columns : (piece + 1) * columns],
            preferred_element_type=jnp.float32,
        )
        partial[piece] = product.reshape(n_head * 2, out_rows, columns)
        for k in range(n_head):
            core_out[piece, k] = partial[
                piece, lax.rem(x + k, n_head) * 2 + sibling
            ].astype(jnp.bfloat16)
        sum_core(piece).start()

    def add_core(piece):
        sum_core(piece).wait_recv()
        for k in range(1, n_head):
            head_out[piece, k - 1] = (
                partial[piece, lax.rem(x + k, n_head) * 2 + c]
                + core_in[piece, k].astype(jnp.float32)
            ).astype(jnp.bfloat16)
            sum_head(piece, k).start()

    for piece in range(pieces):
        project(piece)
        if piece:
            add_core(piece - 1)
    add_core(pieces - 1)
    for piece in range(pieces):
        total = partial[piece, x * 2 + c] + core_in[piece, 0].astype(jnp.float32)
        for k in range(1, n_head):
            sum_head(piece, k).wait_recv()
            total = total + head_in[piece, k - 1].astype(jnp.float32)
        out_ref[:, piece * columns : (piece + 1) * columns] = total.astype(out_ref.dtype)

    own_copy(c).wait_send()
    for b in range(1, levels + 1):
        for i in range(per_share):

            @pl.when(seq_start(b, i))
            def _():
                seq_copy(b, i).wait_send()

            @pl.when(z >= 2 ** (b - 1))
            def _():
                for k in range(1, n_head):
                    head_copy(b, k, i).wait_send()
                for k in range(n_head):
                    core_copy(b, k, i, c).wait_send()

    for piece in range(pieces):
        sum_core(piece).wait_send()
        for k in range(1, n_head):
            sum_head(piece, k).wait_send()


def shards(query_latent, query_rope, latent, key_rope, value_up, out_proj):
    q_dev, heads, width = query_latent.shape
    rope_width = key_rope.shape[0]
    half = latent.shape[0]
    n_seq, n_head = lax.axis_size("seq"), lax.axis_size("head")
    levels = min(4, n_seq // 4 + 1)
    chunk = lanes
    per_share = half // (n_head * chunk)
    chunks = half // chunk
    pack = rope_width * chunk // width
    rows = q_dev * heads
    features = out_proj.shape[1]
    columns = column_width(features, 8 * lanes)
    pieces = features // columns
    out_rows = q_dev // (2 * n_head)
    dims = (n_seq, n_head, levels, heads, q_dev, width, rope_width, chunk, per_share)
    if heads % 8:
        query_latent = query_latent.reshape(rows, width)
    bf16, f32 = jnp.bfloat16, jnp.float32
    dma = pltpu.SemaphoreType.DMA
    others = max(1, n_head - 1)
    return pl.pallas_call(
        functools.partial(kernel, dims),
        out_shape=jax.ShapeDtypeStruct((out_rows, features), bf16),
        in_specs=[pl.BlockSpec(memory_space=pl.ANY)] * 6,
        out_specs=pl.BlockSpec(memory_space=pltpu.VMEM),
        scratch_shapes=[
            pltpu.VMEM((levels + 1, 2, chunks, chunk + pack, width), bf16),
            pltpu.VMEM(query_latent.shape, bf16),
            pltpu.VMEM(query_rope.shape, bf16),
            pltpu.VMEM(key_rope.shape, bf16),
            pltpu.VMEM(value_up.shape, bf16),
            pltpu.VMEM(out_proj.shape, bf16),
            pltpu.VMEM((rows, width), bf16),
            pltpu.VMEM((rows, lanes), f32),
            pltpu.VMEM((rows, rope_width), bf16),
            pltpu.VMEM((rows, lanes), f32),
            pltpu.VMEM((rows, lanes), f32),
            pltpu.VMEM((width // lanes, rows, lanes), f32),
            pltpu.VMEM((q_dev, heads * value_up.shape[2]), bf16),
            pltpu.VMEM((pieces, 2 * n_head, out_rows, columns), f32),
            pltpu.VMEM((pieces, n_head, out_rows, columns), bf16),
            pltpu.VMEM((pieces, n_head, out_rows, columns), bf16),
            pltpu.VMEM((pieces, others, out_rows, columns), bf16),
            pltpu.VMEM((pieces, others, out_rows, columns), bf16),
            dma((chunks + 5,)),
            dma,
            dma,
            dma((levels, per_share)),
            dma((levels, per_share)),
            dma((levels, others, per_share)),
            dma((levels, others, per_share)),
            dma((levels, n_head, per_share)),
            dma((levels, n_head, per_share)),
            dma((pieces,)),
            dma((pieces,)),
            dma((pieces, others)),
            dma((pieces, others)),
        ],
        compiler_params=pltpu.CompilerParams(
            collective_id=0, has_side_effects=True, vmem_limit_bytes=50 * 1024 * 1024
        ),
        cost_estimate=pl.CostEstimate(
            flops=2 * rows * (levels + 1) * 2 * half * (2 * width + rope_width),
            bytes_accessed=2 * (rows * width + out_proj.size),
            transcendentals=rows * (levels + 1) * 2 * half,
        ),
    )(query_latent, query_rope, latent, key_rope, value_up, out_proj)


def solution(mesh):
    placed = (
        P(("grp", "seq"), ("head", "rep"), None),
        P(("grp", "seq"), ("head", "rep")),
        P(("grp", "seq", "rep"), None),
        P(None, ("grp", "seq", "rep")),
        P(("head", "rep"), None, None),
        P(("head", "rep"), None),
    )
    return jax.shard_map(
        shards,
        mesh=mesh,
        in_specs=placed,
        out_specs=P(("grp", "seq", "head", "rep"), None),
        check_vma=False,
    )
```

```python
import functools
import math

import jax
import jax.numpy as jnp
from jax import lax
from jax.experimental import pallas as pl
from jax.experimental.pallas import tpu as pltpu
from jax.sharding import PartitionSpec as P

lanes = 128
masked_score = -1e30
MESH = pl.DeviceIdType.MESH


def tile_rows(rows, most):
    tile = min(rows, most)
    while rows % tile:
        tile -= 8
    return tile


def column_width(columns, most):
    width = most
    while columns % width:
        width -= lanes
    return width


def kernel(
    dims,
    query_hbm,
    query_rope_hbm,
    latent_hbm,
    rope_hbm,
    value_up_hbm,
    out_proj_hbm,
    out_ref,
    keys,
    query_in,
    query_rope_in,
    rope_in,
    value_up,
    out_proj,
    queries,
    rope_wide,
    rope_queries,
    row_max,
    row_sum,
    attended,
    expanded,
    partial,
    core_out,
    core_in,
    head_out,
    head_in,
    local_sem,
    own_send,
    own_recv,
    seq_send,
    seq_recv,
    head_send,
    head_recv,
    core_send,
    core_recv,
    sum_core_send,
    sum_core_recv,
    sum_head_send,
    sum_head_recv,
):
    n_seq, n_head, levels, heads, q_dev, width, rope_width, chunk, per_share = dims
    rows = q_dev * heads
    half = latent_hbm.shape[0]
    chunks = half // chunk
    pack = keys.shape[3] - chunk
    z = lax.axis_index("seq")
    x = lax.axis_index("head")
    c = lax.axis_index("rep")
    sibling = 1 - c
    scale = (width + rope_width) ** (-0.5) * math.log2(math.e)

    latent_loads = [
        pltpu.make_async_copy(
            latent_hbm.at[pl.ds(j * chunk, chunk), :],
            keys.at[0, c, j, pl.ds(0, chunk), :],
            local_sem.at[j],
        )
        for j in range(chunks)
    ]
    rope_load = pltpu.make_async_copy(rope_hbm, rope_in, local_sem.at[chunks])
    query_load = pltpu.make_async_copy(query_hbm, query_in, local_sem.at[chunks + 1])
    query_rope_load = pltpu.make_async_copy(
        query_rope_hbm, query_rope_in, local_sem.at[chunks + 2]
    )
    value_load = pltpu.make_async_copy(value_up_hbm, value_up, local_sem.at[chunks + 3])
    proj_load = pltpu.make_async_copy(out_proj_hbm, out_proj, local_sem.at[chunks + 4])
    rope_load.start()
    for load in latent_loads:
        load.start()
    query_load.start()
    query_rope_load.start()

    hops = sorted({1} | {2 ** (b - 1) for b in range(1, levels)})
    barrier = pltpu.get_barrier_semaphore()
    pl.semaphore_signal(barrier, inc=1, device_id={"rep": sibling}, device_id_type=MESH)
    for k in range(1, n_head):
        pl.semaphore_signal(
            barrier, inc=1, device_id={"head": lax.rem(x + k, n_head)}, device_id_type=MESH
        )
    for hop in hops:

        @pl.when(z >= hop)
        def _():
            pl.semaphore_signal(
                barrier, inc=1, device_id={"seq": z - hop}, device_id_type=MESH
            )

    rope_load.wait()
    for load in latent_loads:
        load.wait()
    value_load.start()
    proj_load.start()
    per_row = width // chunk
    for j in range(chunks):
        for k in range(per_row):
            keys[0, c, j, chunk : chunk + pack, k * chunk : (k + 1) * chunk] = rope_in[
                k * pack : (k + 1) * pack, j * chunk : (j + 1) * chunk
            ]

    targets = n_head
    for hop in hops:
        targets = targets + jnp.where(z + hop < n_seq, 1, 0)
    pl.semaphore_wait(barrier, targets)

    def share(k):
        return lax.rem(x + n_head - k, n_head)

    def place(b, r, k, i):
        return keys.at[b, r, share(k) * per_share + i]

    def seq_copy(b, i):
        hop = 1 if b == 1 else 2 ** (b - 2)
        return pltpu.make_async_remote_copy(
            src_ref=place(b - 1, c, 0, i),
            dst_ref=place(b, c, 0, i),
            send_sem=seq_send.at[b - 1, i],
            recv_sem=seq_recv.at[b - 1, i],
            device_id={"seq": jnp.minimum(z + hop, n_seq - 1)},
            device_id_type=MESH,
        )

    def seq_start(b, i):
        hop = 1 if b == 1 else 2 ** (b - 2)
        return (z + hop < n_seq) & (z >= (0 if b == 1 else 2 ** (b - 2)))

    def head_copy(b, k, i):
        return pltpu.make_async_remote_copy(
            src_ref=place(b, c, 0, i),
            dst_ref=place(b, c, 0, i),
            send_sem=head_send.at[b - 1, k - 1, i],
            recv_sem=head_recv.at[b - 1, k - 1, i],
            device_id={"head": lax.rem(x + k, n_head)},
            device_id_type=MESH,
        )

    def head_arrival(b, k, i):
        return pltpu.make_async_remote_copy(
            src_ref=place(b, c, k, i),
            dst_ref=place(b, c, k, i),
            send_sem=head_send.at[b - 1, k - 1, i],
            recv_sem=head_recv.at[b - 1, k - 1, i],
            device_id={"head": lax.rem(x + k, n_head)},
            device_id_type=MESH,
        )

    def core_copy(b, k, i, r):
        return pltpu.make_async_remote_copy(
            src_ref=place(b, r, k, i),
            dst_ref=place(b, r, k, i),
            send_sem=core_send.at[b - 1, k, i],
            recv_sem=core_recv.at[b - 1, k, i],
            device_id={"rep": sibling},
            device_id_type=MESH,
        )

    def own_copy(r):
        return pltpu.make_async_remote_copy(
            src_ref=keys.at[0, r],
            dst_ref=keys.at[0, r],
            send_sem=own_send,
            recv_sem=own_recv,
            device_id={"rep": sibling},
            device_id_type=MESH,
        )

    def send_on(b, i):
        @pl.when(z >= 2 ** (b - 1))
        def _():
            seq_copy(b, i).wait_recv()
            if b < levels:

                @pl.when(seq_start(b + 1, i))
                def _():
                    seq_copy(b + 1, i).start()

            for k in range(1, n_head):
                head_copy(b, k, i).start()
            core_copy(b, 0, i, c).start()

    def pass_core(b, k, i):
        @pl.when(z >= 2 ** (b - 1))
        def _():
            head_arrival(b, k, i).wait_recv()
            core_copy(b, k, i, c).start()

    for i in range(per_share):

        @pl.when(seq_start(1, i))
        def _():
            seq_copy(1, i).start()

    own_copy(c).start()

    query_load.wait()
    query_rope_load.wait()
    if len(query_in.shape) == 3:
        step_q = q_dev // 4
        for part in range(4):
            queries[part * step_q * heads : (part + 1) * step_q * heads, :] = (
                query_in[part * step_q : (part + 1) * step_q]
                .astype(jnp.float32)
                .reshape(step_q * heads, width)
                .astype(jnp.bfloat16)
            )
        query_source = queries
    else:
        query_source = query_in
    for h in range(heads):
        start = h * rope_width // lanes * lanes
        shift = h * rope_width - start
        piece = query_rope_in[:, start : start + lanes].astype(jnp.float32)
        if shift:
            piece = pltpu.roll(piece, lanes - shift, 1)
        rope_wide[pl.ds(h, q_dev, stride=heads), :] = piece
    rope_queries[...] = rope_wide[:, :rope_width].astype(jnp.bfloat16)

    tile = tile_rows(rows, 512)

    def attend(places, first=False, key_base=None, between=None, after=None):
        def key_rows():
            return jnp.concatenate([keys[b, r, j, :chunk, :] for b, r, j in places], axis=0)

        def key_ropes():
            return jnp.concatenate(
                [
                    jnp.concatenate(
                        [
                            keys[b, r, j, chunk : chunk + pack, k * chunk : (k + 1) * chunk]
                            for k in range(per_row)
                        ],
                        axis=0,
                    )
                    for b, r, j in places
                ],
                axis=1,
            )

        def scores_of(base):
            at = pl.ds(base, tile)
            scores = lax.dot_general(
                query_source[at, :],
                key_rows(),
                (((1,), (1,)), ((), ())),
                preferred_element_type=jnp.float32,
            )
            scores = scores + jnp.dot(
                rope_queries[at, :], key_ropes(), preferred_element_type=jnp.float32
            )
            if key_base is not None:
                key = key_base + lax.broadcasted_iota(jnp.int32, scores.shape, 1)
                row = base + lax.broadcasted_iota(jnp.int32, scores.shape, 0)
                limit = (2 * half - q_dev) + row // heads
                scores = jnp.where(key <= limit, scores, masked_score)
            return scores * scale

        def fold(base, scores):
            at = pl.ds(base, tile)
            top = jnp.max(scores, axis=1, keepdims=True)
            if not first:
                old = row_max[at, :1]
                top = jnp.maximum(top, old)
            weights = jnp.exp2(scores - top)
            part = weights[:, :lanes]
            for k in range(1, weights.shape[1] // lanes):
                part = part + weights[:, k * lanes : (k + 1) * lanes]
            update = jnp.dot(
                weights.astype(jnp.bfloat16), key_rows(), preferred_element_type=jnp.float32
            )
            if first:
                row_sum[at, :] = part
            else:
                factor = jnp.exp2(old - top)
                row_sum[at, :] = row_sum[at, :] * factor + part
            for k in range(width // lanes):
                piece = update[:, k * lanes : (k + 1) * lanes]
                if not first:
                    piece = attended[k, at, :] * factor + piece
                attended[k, at, :] = piece
            row_max[at, :] = jnp.broadcast_to(top, (tile, lanes))

        bases = list(range(0, rows, tile))
        scores = [scores_of(base) for base in bases]
        for n, base in enumerate(bases):
            fold(base, scores[n])
            if n == 0 and between is not None:
                between()
        if after is not None:
            after()

    def attend_shares(b, pieces, between=None):
        @pl.when(z >= 2 ** (b - 1))
        def _():
            for k, i in pieces:
                core_copy(b, k, i, sibling).wait_recv()
            attend(
                [(b, r, share(k) * per_share + i) for r in (c, sibling) for k, i in pieces],
                between=between,
            )

    others = range(1, n_head)
    attend([(0, c, j) for j in range(chunks)], first=True, key_base=c * half)
    send_on(1, 0)
    own_copy(sibling).wait_recv()
    attend([(0, sibling, j) for j in range(chunks)], key_base=sibling * half)
    for i in range(1, per_share):
        send_on(1, i)
    for b in range(1, levels + 1):
        for k in others:
            pass_core(b, k, 0)
        ahead = [(k, 0) for k in others] if per_share > 1 else []
        if b < levels:
            attend_shares(b, [(0, i) for i in range(per_share)])
            send_on(b + 1, 0)
            for k in others:
                for i in range(1, per_share):
                    pass_core(b, k, i)
            attend_shares(b, [(k, i) for k in others for i in range(per_share)])
            for i in range(1, per_share):
                send_on(b + 1, i)
        else:
            attend_shares(b, [(0, i) for i in range(per_share)] + ahead)
            rest = [(k, i) for k in others for i in range(per_share) if (k, i) not in ahead]
            for k, i in rest:
                if i:
                    pass_core(b, k, i)
            attend_shares(b, rest)

    value_load.wait()

    def normalise(step, _):
        at = pl.ds(pl.multiple_of(step * tile, tile), tile)
        inverse = 1.0 / jnp.sum(row_sum[at, :], axis=1, keepdims=True)
        for k in range(width // lanes):
            attended[k, at, :] = attended[k, at, :] * inverse
        return 0

    lax.fori_loop(0, rows // tile, normalise, 0)
    value_width = value_up.shape[2]
    for h in range(heads):
        latent_out = jnp.concatenate(
            [
                attended[k, pl.ds(h, q_dev, stride=heads), :].astype(jnp.bfloat16)
                for k in range(width // lanes)
            ],
            axis=1,
        )
        expanded[:, h * value_width : (h + 1) * value_width] = jnp.dot(
            latent_out, value_up[h], preferred_element_type=jnp.float32
        ).astype(jnp.bfloat16)

    proj_load.wait()
    columns, out_rows = core_out.shape[3], core_out.shape[2]
    pieces = core_out.shape[0]

    def sum_core(piece):
        return pltpu.make_async_remote_copy(
            src_ref=core_out.at[piece],
            dst_ref=core_in.at[piece],
            send_sem=sum_core_send.at[piece],
            recv_sem=sum_core_recv.at[piece],
            device_id={"rep": sibling},
            device_id_type=MESH,
        )

    def sum_head(piece, k):
        return pltpu.make_async_remote_copy(
            src_ref=head_out.at[piece, k - 1],
            dst_ref=head_in.at[piece, k - 1],
            send_sem=sum_head_send.at[piece, k - 1],
            recv_sem=sum_head_recv.at[piece, k - 1],
            device_id={"head": lax.rem(x + k, n_head)},
            device_id_type=MESH,
        )

    def project(piece):
        product = jnp.dot(
            expanded[...],
            out_proj[:, piece * columns : (piece + 1) * columns],
            preferred_element_type=jnp.float32,
        )
        partial[piece] = product.reshape(n_head * 2, out_rows, columns)
        for k in range(n_head):
            core_out[piece, k] = partial[
                piece, lax.rem(x + k, n_head) * 2 + sibling
            ].astype(jnp.bfloat16)
        sum_core(piece).start()

    def add_core(piece):
        sum_core(piece).wait_recv()
        for k in range(1, n_head):
            head_out[piece, k - 1] = (
                partial[piece, lax.rem(x + k, n_head) * 2 + c]
                + core_in[piece, k].astype(jnp.float32)
            ).astype(jnp.bfloat16)
            sum_head(piece, k).start()

    for piece in range(pieces):
        project(piece)
        if piece:
            add_core(piece - 1)
    add_core(pieces - 1)
    for piece in range(pieces):
        total = partial[piece, x * 2 + c] + core_in[piece, 0].astype(jnp.float32)
        for k in range(1, n_head):
            sum_head(piece, k).wait_recv()
            total = total + head_in[piece, k - 1].astype(jnp.float32)
        out_ref[:, piece * columns : (piece + 1) * columns] = total.astype(out_ref.dtype)

    own_copy(c).wait_send()
    for b in range(1, levels + 1):
        for i in range(per_share):

            @pl.when(seq_start(b, i))
            def _():
                seq_copy(b, i).wait_send()

            @pl.when(z >= 2 ** (b - 1))
            def _():
                for k in range(1, n_head):
                    head_copy(b, k, i).wait_send()
                for k in range(n_head):
                    core_copy(b, k, i, c).wait_send()

    for piece in range(pieces):
        sum_core(piece).wait_send()
        for k in range(1, n_head):
            sum_head(piece, k).wait_send()


def shards(query_latent, query_rope, latent, key_rope, value_up, out_proj):
    q_dev, heads, width = query_latent.shape
    rope_width = key_rope.shape[0]
    half = latent.shape[0]
    n_seq, n_head = lax.axis_size("seq"), lax.axis_size("head")
    levels = min(4, n_seq // 4 + 1)
    chunk = lanes
    per_share = half // (n_head * chunk)
    chunks = half // chunk
    pack = rope_width * chunk // width
    rows = q_dev * heads
    features = out_proj.shape[1]
    columns = column_width(features, 8 * lanes)
    pieces = features // columns
    out_rows = q_dev // (2 * n_head)
    dims = (n_seq, n_head, levels, heads, q_dev, width, rope_width, chunk, per_share)
    if heads % 8:
        query_latent = query_latent.reshape(rows, width)
    bf16, f32 = jnp.bfloat16, jnp.float32
    dma = pltpu.SemaphoreType.DMA
    others = max(1, n_head - 1)
    return pl.pallas_call(
        functools.partial(kernel, dims),
        out_shape=jax.ShapeDtypeStruct((out_rows, features), bf16),
        in_specs=[pl.BlockSpec(memory_space=pl.ANY)] * 6,
        out_specs=pl.BlockSpec(memory_space=pltpu.VMEM),
        scratch_shapes=[
            pltpu.VMEM((levels + 1, 2, chunks, chunk + pack, width), bf16),
            pltpu.VMEM(query_latent.shape, bf16),
            pltpu.VMEM(query_rope.shape, bf16),
            pltpu.VMEM(key_rope.shape, bf16),
            pltpu.VMEM(value_up.shape, bf16),
            pltpu.VMEM(out_proj.shape, bf16),
            pltpu.VMEM((rows, width), bf16),
            pltpu.VMEM((rows, lanes), f32),
            pltpu.VMEM((rows, rope_width), bf16),
            pltpu.VMEM((rows, lanes), f32),
            pltpu.VMEM((rows, lanes), f32),
            pltpu.VMEM((width // lanes, rows, lanes), f32),
            pltpu.VMEM((q_dev, heads * value_up.shape[2]), bf16),
            pltpu.VMEM((pieces, 2 * n_head, out_rows, columns), f32),
            pltpu.VMEM((pieces, n_head, out_rows, columns), bf16),
            pltpu.VMEM((pieces, n_head, out_rows, columns), bf16),
            pltpu.VMEM((pieces, others, out_rows, columns), bf16),
            pltpu.VMEM((pieces, others, out_rows, columns), bf16),
            dma((chunks + 5,)),
            dma,
            dma,
            dma((levels, per_share)),
            dma((levels, per_share)),
            dma((levels, others, per_share)),
            dma((levels, others, per_share)),
            dma((levels, n_head, per_share)),
            dma((levels, n_head, per_share)),
            dma((pieces,)),
            dma((pieces,)),
            dma((pieces, others)),
            dma((pieces, others)),
        ],
        compiler_params=pltpu.CompilerParams(
            collective_id=0, has_side_effects=True, vmem_limit_bytes=63 * 1024 * 1024
        ),
        cost_estimate=pl.CostEstimate(
            flops=2 * rows * (levels + 1) * 2 * half * (2 * width + rope_width),
            bytes_accessed=2 * (rows * width + out_proj.size),
            transcendentals=rows * (levels + 1) * 2 * half,
        ),
    )(query_latent, query_rope, latent, key_rope, value_up, out_proj)


def solution(mesh):
    placed = (
        P(("grp", "seq"), ("head", "rep"), None),
        P(("grp", "seq"), ("head", "rep")),
        P(("grp", "seq", "rep"), None),
        P(None, ("grp", "seq", "rep")),
        P(("head", "rep"), None, None),
        P(("head", "rep"), None),
    )
    return jax.shard_map(
        shards,
        mesh=mesh,
        in_specs=placed,
        out_specs=P(("grp", "seq", "head", "rep"), None),
        check_vma=False,
    )
```

```python
import functools
import math

import jax
import jax.numpy as jnp
from jax import lax
from jax.experimental import pallas as pl
from jax.experimental.pallas import tpu as pltpu
from jax.sharding import PartitionSpec as P

lanes = 128
masked_score = -1e30
MESH = pl.DeviceIdType.MESH


def tile_rows(rows, most):
    tile = min(rows, most)
    while rows % tile:
        tile -= 8
    return tile


def column_width(columns, most):
    width = most
    while columns % width:
        width -= lanes
    return width


def kernel(
    dims,
    query_hbm,
    query_rope_hbm,
    latent_hbm,
    rope_hbm,
    value_up_hbm,
    out_proj_hbm,
    out_ref,
    keys,
    query_in,
    query_rope_in,
    rope_in,
    value_up,
    out_proj,
    queries,
    rope_wide,
    keys_across,
    row_max,
    row_sum,
    attended,
    expanded,
    partial,
    core_out,
    core_in,
    head_out,
    head_in,
    local_sem,
    own_send,
    own_recv,
    seq_send,
    seq_recv,
    head_send,
    head_recv,
    core_send,
    core_recv,
    sum_core_send,
    sum_core_recv,
    sum_head_send,
    sum_head_recv,
):
    n_seq, n_head, levels, heads, q_dev, width, rope_width, chunk, per_share = dims
    rows = q_dev * heads
    half = latent_hbm.shape[0]
    chunks = half // chunk
    pack = keys.shape[3] - chunk
    z = lax.axis_index("seq")
    x = lax.axis_index("head")
    c = lax.axis_index("rep")
    sibling = 1 - c
    scale = (width + rope_width) ** (-0.5) * math.log2(math.e)

    latent_loads = [
        pltpu.make_async_copy(
            latent_hbm.at[pl.ds(j * chunk, chunk), :],
            keys.at[0, c, j, pl.ds(0, chunk), :],
            local_sem.at[j],
        )
        for j in range(chunks)
    ]
    rope_load = pltpu.make_async_copy(rope_hbm, rope_in, local_sem.at[chunks])
    query_load = pltpu.make_async_copy(query_hbm, query_in, local_sem.at[chunks + 1])
    query_rope_load = pltpu.make_async_copy(
        query_rope_hbm, query_rope_in, local_sem.at[chunks + 2]
    )
    value_load = pltpu.make_async_copy(value_up_hbm, value_up, local_sem.at[chunks + 3])
    proj_load = pltpu.make_async_copy(out_proj_hbm, out_proj, local_sem.at[chunks + 4])
    rope_load.start()
    for load in latent_loads:
        load.start()
    query_load.start()
    query_rope_load.start()

    hops = sorted({1} | {2 ** (b - 1) for b in range(1, levels)})
    barrier = pltpu.get_barrier_semaphore()
    pl.semaphore_signal(barrier, inc=1, device_id={"rep": sibling}, device_id_type=MESH)
    for k in range(1, n_head):
        pl.semaphore_signal(
            barrier, inc=1, device_id={"head": lax.rem(x + k, n_head)}, device_id_type=MESH
        )
    for hop in hops:

        @pl.when(z >= hop)
        def _():
            pl.semaphore_signal(
                barrier, inc=1, device_id={"seq": z - hop}, device_id_type=MESH
            )

    rope_load.wait()
    for load in latent_loads:
        load.wait()
    value_load.start()
    proj_load.start()
    per_row = width // chunk
    for j in range(chunks):
        for k in range(per_row):
            keys[0, c, j, chunk : chunk + pack, k * chunk : (k + 1) * chunk] = rope_in[
                k * pack : (k + 1) * pack, j * chunk : (j + 1) * chunk
            ]

    targets = n_head
    for hop in hops:
        targets = targets + jnp.where(z + hop < n_seq, 1, 0)
    pl.semaphore_wait(barrier, targets)

    def share(k):
        return lax.rem(x + n_head - k, n_head)

    def place(b, r, k, i):
        return keys.at[b, r, share(k) * per_share + i]

    def seq_copy(b, i):
        hop = 1 if b == 1 else 2 ** (b - 2)
        return pltpu.make_async_remote_copy(
            src_ref=place(b - 1, c, 0, i),
            dst_ref=place(b, c, 0, i),
            send_sem=seq_send.at[b - 1, i],
            recv_sem=seq_recv.at[b - 1, i],
            device_id={"seq": jnp.minimum(z + hop, n_seq - 1)},
            device_id_type=MESH,
        )

    def seq_start(b, i):
        hop = 1 if b == 1 else 2 ** (b - 2)
        return (z + hop < n_seq) & (z >= (0 if b == 1 else 2 ** (b - 2)))

    def head_copy(b, k, i):
        return pltpu.make_async_remote_copy(
            src_ref=place(b, c, 0, i),
            dst_ref=place(b, c, 0, i),
            send_sem=head_send.at[b - 1, k - 1, i],
            recv_sem=head_recv.at[b - 1, k - 1, i],
            device_id={"head": lax.rem(x + k, n_head)},
            device_id_type=MESH,
        )

    def head_arrival(b, k, i):
        return pltpu.make_async_remote_copy(
            src_ref=place(b, c, k, i),
            dst_ref=place(b, c, k, i),
            send_sem=head_send.at[b - 1, k - 1, i],
            recv_sem=head_recv.at[b - 1, k - 1, i],
            device_id={"head": lax.rem(x + k, n_head)},
            device_id_type=MESH,
        )

    def core_copy(b, k, i, r):
        return pltpu.make_async_remote_copy(
            src_ref=place(b, r, k, i),
            dst_ref=place(b, r, k, i),
            send_sem=core_send.at[b - 1, k, i],
            recv_sem=core_recv.at[b - 1, k, i],
            device_id={"rep": sibling},
            device_id_type=MESH,
        )

    def own_copy(r):
        return pltpu.make_async_remote_copy(
            src_ref=keys.at[0, r],
            dst_ref=keys.at[0, r],
            send_sem=own_send,
            recv_sem=own_recv,
            device_id={"rep": sibling},
            device_id_type=MESH,
        )

    def send_on(b, i):
        @pl.when(z >= 2 ** (b - 1))
        def _():
            seq_copy(b, i).wait_recv()
            core_copy(b, 0, i, c).start()
            for k in range(1, n_head):
                head_copy(b, k, i).start()
            if b < levels:

                @pl.when(seq_start(b + 1, i))
                def _():
                    seq_copy(b + 1, i).start()

    def pass_core(b, k, i):
        @pl.when(z >= 2 ** (b - 1))
        def _():
            head_arrival(b, k, i).wait_recv()
            core_copy(b, k, i, c).start()

    own_copy(c).start()
    for i in range(per_share):

        @pl.when(seq_start(1, i))
        def _():
            seq_copy(1, i).start()

    query_load.wait()
    query_rope_load.wait()
    if len(query_in.shape) == 3:
        step_q = q_dev // 4
        for part in range(4):
            queries[part * step_q * heads : (part + 1) * step_q * heads, :width] = (
                query_in[part * step_q : (part + 1) * step_q]
                .astype(jnp.float32)
                .reshape(step_q * heads, width)
                .astype(jnp.bfloat16)
            )
    else:
        queries[:, :width] = query_in[...]
    for h in range(heads):
        start = h * rope_width // lanes * lanes
        shift = h * rope_width - start
        piece = query_rope_in[:, start : start + lanes].astype(jnp.float32)
        if shift:
            piece = pltpu.roll(piece, lanes - shift, 1)
        rope_wide[pl.ds(h, q_dev, stride=heads), :] = piece
    queries[:, width:] = rope_wide[:, :rope_width].astype(jnp.bfloat16)

    tile = tile_rows(rows, 512)

    def attend(places, first=False, key_base=None, between=None):
        def key_rows():
            return jnp.concatenate([keys[b, r, j, :chunk, :] for b, r, j in places], axis=0)

        def key_ropes():
            return jnp.concatenate(
                [
                    jnp.concatenate(
                        [
                            keys[b, r, j, chunk : chunk + pack, k * chunk : (k + 1) * chunk]
                            for k in range(per_row)
                        ],
                        axis=0,
                    )
                    for b, r, j in places
                ],
                axis=1,
            )

        count = len(places) * chunk
        keys_across[:width, :count] = key_rows().T
        keys_across[width:, :count] = key_ropes()

        def scores_of(base):
            at = pl.ds(base, tile)
            scores = jnp.dot(
                queries[at, :], keys_across[:, :count], preferred_element_type=jnp.float32
            )
            if key_base is not None:
                key = key_base + lax.broadcasted_iota(jnp.int32, scores.shape, 1)
                row = base + lax.broadcasted_iota(jnp.int32, scores.shape, 0)
                limit = (2 * half - q_dev) + row // heads
                scores = jnp.where(key <= limit, scores, masked_score)
            return scores * scale

        def fold(base, scores):
            at = pl.ds(base, tile)
            top = jnp.max(scores, axis=1, keepdims=True)
            if not first:
                old = row_max[at, :1]
                top = jnp.maximum(top, old)
            weights = jnp.exp2(scores - top)
            part = weights[:, :lanes]
            for k in range(1, weights.shape[1] // lanes):
                part = part + weights[:, k * lanes : (k + 1) * lanes]
            update = jnp.dot(
                weights.astype(jnp.bfloat16), key_rows(), preferred_element_type=jnp.float32
            )
            if first:
                row_sum[at, :] = part
            else:
                factor = jnp.exp2(old - top)
                row_sum[at, :] = row_sum[at, :] * factor + part
            for k in range(width // lanes):
                piece = update[:, k * lanes : (k + 1) * lanes]
                if not first:
                    piece = attended[k, at, :] * factor + piece
                attended[k, at, :] = piece
            row_max[at, :] = jnp.broadcast_to(top, (tile, lanes))

        bases = list(range(0, rows, tile))
        scores = [scores_of(base) for base in bases]
        for n, base in enumerate(bases):
            fold(base, scores[n])
            if n == 0 and between is not None:
                between()

    def attend_shares(b, pieces, between=None):
        @pl.when(z >= 2 ** (b - 1))
        def _():
            for k, i in pieces:
                core_copy(b, k, i, sibling).wait_recv()
            attend(
                [(b, r, share(k) * per_share + i) for r in (c, sibling) for k, i in pieces],
                between=between,
            )

    others = range(1, n_head)

    def later_arrivals(b):
        for i in range(1, per_share):
            send_on(b, i)

    attend([(0, c, j) for j in range(chunks)], first=True, key_base=c * half)
    send_on(1, 0)
    own_copy(sibling).wait_recv()
    attend(
        [(0, sibling, j) for j in range(chunks)],
        key_base=sibling * half,
        between=lambda: later_arrivals(1),
    )
    for b in range(1, levels + 1):
        for k in others:
            pass_core(b, k, 0)
        ahead = [(k, 0) for k in others] if per_share > 1 else []
        if b < levels:
            attend_shares(
                b, [(0, i) for i in range(per_share)], between=lambda: send_on(b + 1, 0)
            )
            for k in others:
                for i in range(1, per_share):
                    pass_core(b, k, i)
            attend_shares(
                b,
                [(k, i) for k in others for i in range(per_share)],
                between=lambda: later_arrivals(b + 1),
            )
        else:
            attend_shares(b, [(0, i) for i in range(per_share)] + ahead)
            rest = [(k, i) for k in others for i in range(per_share) if (k, i) not in ahead]
            for k, i in rest:
                if i:
                    pass_core(b, k, i)
            attend_shares(b, rest)

    value_load.wait()

    def normalise(step, _):
        at = pl.ds(pl.multiple_of(step * tile, tile), tile)
        inverse = 1.0 / jnp.sum(row_sum[at, :], axis=1, keepdims=True)
        for k in range(width // lanes):
            attended[k, at, :] = attended[k, at, :] * inverse
        return 0

    lax.fori_loop(0, rows // tile, normalise, 0)
    value_width = value_up.shape[2]
    for h in range(heads):
        latent_out = jnp.concatenate(
            [
                attended[k, pl.ds(h, q_dev, stride=heads), :].astype(jnp.bfloat16)
                for k in range(width // lanes)
            ],
            axis=1,
        )
        expanded[:, h * value_width : (h + 1) * value_width] = jnp.dot(
            latent_out, value_up[h], preferred_element_type=jnp.float32
        ).astype(jnp.bfloat16)

    proj_load.wait()
    columns, out_rows = core_out.shape[3], core_out.shape[2]
    pieces = core_out.shape[0]

    def sum_core(piece):
        return pltpu.make_async_remote_copy(
            src_ref=core_out.at[piece],
            dst_ref=core_in.at[piece],
            send_sem=sum_core_send.at[piece],
            recv_sem=sum_core_recv.at[piece],
            device_id={"rep": sibling},
            device_id_type=MESH,
        )

    def sum_head(piece, k):
        return pltpu.make_async_remote_copy(
            src_ref=head_out.at[piece, k - 1],
            dst_ref=head_in.at[piece, k - 1],
            send_sem=sum_head_send.at[piece, k - 1],
            recv_sem=sum_head_recv.at[piece, k - 1],
            device_id={"head": lax.rem(x + k, n_head)},
            device_id_type=MESH,
        )

    def project(piece):
        product = jnp.dot(
            expanded[...],
            out_proj[:, piece * columns : (piece + 1) * columns],
            preferred_element_type=jnp.float32,
        )
        partial[piece] = product.reshape(n_head * 2, out_rows, columns)
        for k in range(n_head):
            core_out[piece, k] = partial[
                piece, lax.rem(x + k, n_head) * 2 + sibling
            ].astype(jnp.bfloat16)
        sum_core(piece).start()

    def add_core(piece):
        sum_core(piece).wait_recv()
        for k in range(1, n_head):
            head_out[piece, k - 1] = (
                partial[piece, lax.rem(x + k, n_head) * 2 + c]
                + core_in[piece, k].astype(jnp.float32)
            ).astype(jnp.bfloat16)
            sum_head(piece, k).start()

    for piece in range(pieces):
        project(piece)
        if piece:
            add_core(piece - 1)
    add_core(pieces - 1)
    for piece in range(pieces):
        total = partial[piece, x * 2 + c] + core_in[piece, 0].astype(jnp.float32)
        for k in range(1, n_head):
            sum_head(piece, k).wait_recv()
            total = total + head_in[piece, k - 1].astype(jnp.float32)
        out_ref[:, piece * columns : (piece + 1) * columns] = total.astype(out_ref.dtype)

    own_copy(c).wait_send()
    for b in range(1, levels + 1):
        for i in range(per_share):

            @pl.when(seq_start(b, i))
            def _():
                seq_copy(b, i).wait_send()

            @pl.when(z >= 2 ** (b - 1))
            def _():
                for k in range(1, n_head):
                    head_copy(b, k, i).wait_send()
                for k in range(n_head):
                    core_copy(b, k, i, c).wait_send()

    for piece in range(pieces):
        sum_core(piece).wait_send()
        for k in range(1, n_head):
            sum_head(piece, k).wait_send()


def shards(query_latent, query_rope, latent, key_rope, value_up, out_proj):
    q_dev, heads, width = query_latent.shape
    rope_width = key_rope.shape[0]
    half = latent.shape[0]
    n_seq, n_head = lax.axis_size("seq"), lax.axis_size("head")
    levels = min(4, n_seq // 4 + 1)
    chunk = lanes
    per_share = half // (n_head * chunk)
    chunks = half // chunk
    pack = rope_width * chunk // width
    rows = q_dev * heads
    features = out_proj.shape[1]
    columns = column_width(features, 8 * lanes)
    pieces = features // columns
    out_rows = q_dev // (2 * n_head)
    dims = (n_seq, n_head, levels, heads, q_dev, width, rope_width, chunk, per_share)
    if heads % 8:
        query_latent = query_latent.reshape(rows, width)
    bf16, f32 = jnp.bfloat16, jnp.float32
    dma = pltpu.SemaphoreType.DMA
    others = max(1, n_head - 1)
    return pl.pallas_call(
        functools.partial(kernel, dims),
        out_shape=jax.ShapeDtypeStruct((out_rows, features), bf16),
        in_specs=[pl.BlockSpec(memory_space=pl.ANY)] * 6,
        out_specs=pl.BlockSpec(memory_space=pltpu.VMEM),
        scratch_shapes=[
            pltpu.VMEM((levels + 1, 2, chunks, chunk + pack, width), bf16),
            pltpu.VMEM(query_latent.shape, bf16),
            pltpu.VMEM(query_rope.shape, bf16),
            pltpu.VMEM(key_rope.shape, bf16),
            pltpu.VMEM(value_up.shape, bf16),
            pltpu.VMEM(out_proj.shape, bf16),
            pltpu.VMEM((rows, width + rope_width), bf16),
            pltpu.VMEM((rows, lanes), f32),
            pltpu.VMEM((width + rope_width, 2 * half), bf16),
            pltpu.VMEM((rows, lanes), f32),
            pltpu.VMEM((rows, lanes), f32),
            pltpu.VMEM((width // lanes, rows, lanes), f32),
            pltpu.VMEM((q_dev, heads * value_up.shape[2]), bf16),
            pltpu.VMEM((pieces, 2 * n_head, out_rows, columns), f32),
            pltpu.VMEM((pieces, n_head, out_rows, columns), bf16),
            pltpu.VMEM((pieces, n_head, out_rows, columns), bf16),
            pltpu.VMEM((pieces, others, out_rows, columns), bf16),
            pltpu.VMEM((pieces, others, out_rows, columns), bf16),
            dma((chunks + 5,)),
            dma,
            dma,
            dma((levels, per_share)),
            dma((levels, per_share)),
            dma((levels, others, per_share)),
            dma((levels, others, per_share)),
            dma((levels, n_head, per_share)),
            dma((levels, n_head, per_share)),
            dma((pieces,)),
            dma((pieces,)),
            dma((pieces, others)),
            dma((pieces, others)),
        ],
        compiler_params=pltpu.CompilerParams(
            collective_id=0, has_side_effects=True, vmem_limit_bytes=63 * 1024 * 1024
        ),
        cost_estimate=pl.CostEstimate(
            flops=2 * rows * (levels + 1) * 2 * half * (2 * width + rope_width),
            bytes_accessed=2 * (rows * width + out_proj.size),
            transcendentals=rows * (levels + 1) * 2 * half,
        ),
    )(query_latent, query_rope, latent, key_rope, value_up, out_proj)


def solution(mesh):
    placed = (
        P(("grp", "seq"), ("head", "rep"), None),
        P(("grp", "seq"), ("head", "rep")),
        P(("grp", "seq", "rep"), None),
        P(None, ("grp", "seq", "rep")),
        P(("head", "rep"), None, None),
        P(("head", "rep"), None),
    )
    return jax.shard_map(
        shards,
        mesh=mesh,
        in_specs=placed,
        out_specs=P(("grp", "seq", "head", "rep"), None),
        check_vma=False,
    )
```

```python
import functools
import math

import jax
import jax.numpy as jnp
from jax import lax
from jax.experimental import pallas as pl
from jax.experimental.pallas import tpu as pltpu
from jax.sharding import PartitionSpec as P

lanes = 128
masked_score = -1e30
MESH = pl.DeviceIdType.MESH


def tile_rows(rows, most):
    tile = min(rows, most)
    while rows % tile:
        tile -= 8
    return tile


def part_rows(chunk, pack):
    first = chunk // 2
    return ((0, first), (first, chunk + pack - first))


def column_width(columns, most):
    width = most
    while columns % width:
        width -= lanes
    return width


def kernel(
    dims,
    query_hbm,
    query_rope_hbm,
    latent_hbm,
    rope_hbm,
    value_up_hbm,
    out_proj_hbm,
    out_ref,
    keys,
    query_in,
    query_rope_in,
    rope_in,
    value_up,
    out_proj,
    queries,
    rope_wide,
    keys_across,
    row_max,
    row_sum,
    attended,
    expanded,
    partial,
    core_out,
    core_in,
    head_out,
    head_in,
    local_sem,
    own_send,
    own_recv,
    seq_send,
    seq_recv,
    head_send,
    head_recv,
    core_send,
    core_recv,
    sum_core_send,
    sum_core_recv,
    sum_head_send,
    sum_head_recv,
):
    n_seq, n_head, levels, heads, q_dev, width, rope_width, chunk, per_share = dims
    rows = q_dev * heads
    half = latent_hbm.shape[0]
    chunks = half // chunk
    pack = keys.shape[3] - chunk
    z = lax.axis_index("seq")
    x = lax.axis_index("head")
    c = lax.axis_index("rep")
    sibling = 1 - c
    scale = (width + rope_width) ** (-0.5) * math.log2(math.e)

    latent_loads = [
        pltpu.make_async_copy(
            latent_hbm.at[pl.ds(j * chunk, chunk), :],
            keys.at[0, c, j, pl.ds(0, chunk), :],
            local_sem.at[j],
        )
        for j in range(chunks)
    ]
    rope_load = pltpu.make_async_copy(rope_hbm, rope_in, local_sem.at[chunks])
    query_load = pltpu.make_async_copy(query_hbm, query_in, local_sem.at[chunks + 1])
    query_rope_load = pltpu.make_async_copy(
        query_rope_hbm, query_rope_in, local_sem.at[chunks + 2]
    )
    value_load = pltpu.make_async_copy(value_up_hbm, value_up, local_sem.at[chunks + 3])
    proj_load = pltpu.make_async_copy(out_proj_hbm, out_proj, local_sem.at[chunks + 4])
    rope_load.start()
    for load in latent_loads:
        load.start()
    query_load.start()
    query_rope_load.start()

    hops = sorted({1} | {2 ** (b - 1) for b in range(1, levels)})
    barrier = pltpu.get_barrier_semaphore()
    pl.semaphore_signal(barrier, inc=1, device_id={"rep": sibling}, device_id_type=MESH)
    for k in range(1, n_head):
        pl.semaphore_signal(
            barrier, inc=1, device_id={"head": lax.rem(x + k, n_head)}, device_id_type=MESH
        )
    for hop in hops:

        @pl.when(z >= hop)
        def _():
            pl.semaphore_signal(
                barrier, inc=1, device_id={"seq": z - hop}, device_id_type=MESH
            )

    rope_load.wait()
    for load in latent_loads:
        load.wait()
    value_load.start()
    proj_load.start()
    per_row = width // chunk
    for j in range(chunks):
        for k in range(per_row):
            keys[0, c, j, chunk : chunk + pack, k * chunk : (k + 1) * chunk] = rope_in[
                k * pack : (k + 1) * pack, j * chunk : (j + 1) * chunk
            ]

    targets = n_head
    for hop in hops:
        targets = targets + jnp.where(z + hop < n_seq, 1, 0)
    pl.semaphore_wait(barrier, targets)

    def share(k):
        return lax.rem(x + n_head - k, n_head)

    parts = part_rows(chunk, pack)

    def place(b, r, k, i, part):
        start, count = parts[part]
        return keys.at[b, r, share(k) * per_share + i, pl.ds(start, count), :]

    def seq_copy(b, i, part):
        hop = 1 if b == 1 else 2 ** (b - 2)
        return pltpu.make_async_remote_copy(
            src_ref=place(b - 1, c, 0, i, part),
            dst_ref=place(b, c, 0, i, part),
            send_sem=seq_send.at[b - 1, i, part],
            recv_sem=seq_recv.at[b - 1, i, part],
            device_id={"seq": jnp.minimum(z + hop, n_seq - 1)},
            device_id_type=MESH,
        )

    def seq_start(b, i):
        hop = 1 if b == 1 else 2 ** (b - 2)
        return (z + hop < n_seq) & (z >= (0 if b == 1 else 2 ** (b - 2)))

    def head_copy(b, k, i, part):
        return pltpu.make_async_remote_copy(
            src_ref=place(b, c, 0, i, part),
            dst_ref=place(b, c, 0, i, part),
            send_sem=head_send.at[b - 1, k - 1, i, part],
            recv_sem=head_recv.at[b - 1, k - 1, i, part],
            device_id={"head": lax.rem(x + k, n_head)},
            device_id_type=MESH,
        )

    def head_arrival(b, k, i, part):
        return pltpu.make_async_remote_copy(
            src_ref=place(b, c, k, i, part),
            dst_ref=place(b, c, k, i, part),
            send_sem=head_send.at[b - 1, k - 1, i, part],
            recv_sem=head_recv.at[b - 1, k - 1, i, part],
            device_id={"head": lax.rem(x + k, n_head)},
            device_id_type=MESH,
        )

    def core_copy(b, k, i, r, part):
        return pltpu.make_async_remote_copy(
            src_ref=place(b, r, k, i, part),
            dst_ref=place(b, r, k, i, part),
            send_sem=core_send.at[b - 1, k, i, part],
            recv_sem=core_recv.at[b - 1, k, i, part],
            device_id={"rep": sibling},
            device_id_type=MESH,
        )

    def own_copy(r):
        return pltpu.make_async_remote_copy(
            src_ref=keys.at[0, r],
            dst_ref=keys.at[0, r],
            send_sem=own_send,
            recv_sem=own_recv,
            device_id={"rep": sibling},
            device_id_type=MESH,
        )

    def send_on(b, i):
        @pl.when(z >= 2 ** (b - 1))
        def _():
            for part in range(len(parts)):
                seq_copy(b, i, part).wait_recv()
                for k in range(1, n_head):
                    head_copy(b, k, i, part).start()
                if b < levels:

                    @pl.when(seq_start(b + 1, i))
                    def _():
                        seq_copy(b + 1, i, part).start()

                core_copy(b, 0, i, c, part).start()

    def pass_core(b, k, i):
        @pl.when(z >= 2 ** (b - 1))
        def _():
            for part in range(len(parts)):
                head_arrival(b, k, i, part).wait_recv()
                core_copy(b, k, i, c, part).start()

    own_copy(c).start()
    for i in range(per_share):

        @pl.when(seq_start(1, i))
        def _():
            for part in range(len(parts)):
                seq_copy(1, i, part).start()

    query_load.wait()
    query_rope_load.wait()
    if len(query_in.shape) == 3:
        step_q = q_dev // 4
        for part in range(4):
            queries[part * step_q * heads : (part + 1) * step_q * heads, :width] = (
                query_in[part * step_q : (part + 1) * step_q]
                .astype(jnp.float32)
                .reshape(step_q * heads, width)
                .astype(jnp.bfloat16)
            )
    else:
        queries[:, :width] = query_in[...]
    for h in range(heads):
        start = h * rope_width // lanes * lanes
        shift = h * rope_width - start
        piece = query_rope_in[:, start : start + lanes].astype(jnp.float32)
        if shift:
            piece = pltpu.roll(piece, lanes - shift, 1)
        rope_wide[pl.ds(h, q_dev, stride=heads), :] = piece
    queries[:, width:] = rope_wide[:, :rope_width].astype(jnp.bfloat16)

    tile = tile_rows(rows, 512)

    def attend(places, first=False, key_base=None, between=None):
        def key_rows():
            return jnp.concatenate([keys[b, r, j, :chunk, :] for b, r, j in places], axis=0)

        def key_ropes():
            return jnp.concatenate(
                [
                    jnp.concatenate(
                        [
                            keys[b, r, j, chunk : chunk + pack, k * chunk : (k + 1) * chunk]
                            for k in range(per_row)
                        ],
                        axis=0,
                    )
                    for b, r, j in places
                ],
                axis=1,
            )

        count = len(places) * chunk
        keys_across[:width, :count] = key_rows().T
        keys_across[width:, :count] = key_ropes()

        def scores_of(base):
            at = pl.ds(base, tile)
            scores = jnp.dot(
                queries[at, :], keys_across[:, :count], preferred_element_type=jnp.float32
            )
            if key_base is not None:
                key = key_base + lax.broadcasted_iota(jnp.int32, scores.shape, 1)
                row = base + lax.broadcasted_iota(jnp.int32, scores.shape, 0)
                limit = (2 * half - q_dev) + row // heads
                scores = jnp.where(key <= limit, scores, masked_score)
            return scores * scale

        def fold(base, scores):
            at = pl.ds(base, tile)
            top = jnp.max(scores, axis=1, keepdims=True)
            if not first:
                old = row_max[at, :1]
                top = jnp.maximum(top, old)
            weights = jnp.exp2(scores - top)
            part = weights[:, :lanes]
            for k in range(1, weights.shape[1] // lanes):
                part = part + weights[:, k * lanes : (k + 1) * lanes]
            update = jnp.dot(
                weights.astype(jnp.bfloat16), key_rows(), preferred_element_type=jnp.float32
            )
            if first:
                row_sum[at, :] = part
            else:
                factor = jnp.exp2(old - top)
                row_sum[at, :] = row_sum[at, :] * factor + part
            for k in range(width // lanes):
                piece = update[:, k * lanes : (k + 1) * lanes]
                if not first:
                    piece = attended[k, at, :] * factor + piece
                attended[k, at, :] = piece
            row_max[at, :] = jnp.broadcast_to(top, (tile, lanes))

        bases = list(range(0, rows, tile))
        scores = [scores_of(base) for base in bases]
        for n, base in enumerate(bases):
            fold(base, scores[n])
            if n == 0 and between is not None:
                between()

    def attend_shares(b, pieces, between=None):
        @pl.when(z >= 2 ** (b - 1))
        def _():
            for k, i in pieces:
                for part in range(len(parts)):
                    core_copy(b, k, i, sibling, part).wait_recv()
            attend(
                [(b, r, share(k) * per_share + i) for r in (c, sibling) for k, i in pieces],
                between=between,
            )

    others = range(1, n_head)

    def later_arrivals(b):
        for i in range(1, per_share):
            send_on(b, i)

    attend([(0, c, j) for j in range(chunks)], first=True, key_base=c * half)
    send_on(1, 0)
    own_copy(sibling).wait_recv()
    attend(
        [(0, sibling, j) for j in range(chunks)],
        key_base=sibling * half,
        between=lambda: later_arrivals(1),
    )
    for b in range(1, levels + 1):
        for k in others:
            pass_core(b, k, 0)
        ahead = [(k, 0) for k in others] if per_share > 1 else []
        if b < levels:
            attend_shares(
                b, [(0, i) for i in range(per_share)], between=lambda: send_on(b + 1, 0)
            )
            for k in others:
                for i in range(1, per_share):
                    pass_core(b, k, i)
            attend_shares(
                b,
                [(k, i) for k in others for i in range(per_share)],
                between=lambda: later_arrivals(b + 1),
            )
        else:
            attend_shares(b, [(0, i) for i in range(per_share)] + ahead)
            rest = [(k, i) for k in others for i in range(per_share) if (k, i) not in ahead]
            for k, i in rest:
                if i:
                    pass_core(b, k, i)
            attend_shares(b, rest)

    value_load.wait()

    def normalise(step, _):
        at = pl.ds(pl.multiple_of(step * tile, tile), tile)
        inverse = 1.0 / jnp.sum(row_sum[at, :], axis=1, keepdims=True)
        for k in range(width // lanes):
            attended[k, at, :] = attended[k, at, :] * inverse
        return 0

    lax.fori_loop(0, rows // tile, normalise, 0)
    value_width = value_up.shape[2]
    for h in range(heads):
        latent_out = jnp.concatenate(
            [
                attended[k, pl.ds(h, q_dev, stride=heads), :].astype(jnp.bfloat16)
                for k in range(width // lanes)
            ],
            axis=1,
        )
        expanded[:, h * value_width : (h + 1) * value_width] = jnp.dot(
            latent_out, value_up[h], preferred_element_type=jnp.float32
        ).astype(jnp.bfloat16)

    proj_load.wait()
    columns, out_rows = core_out.shape[3], core_out.shape[2]
    pieces = core_out.shape[0]

    def sum_core(piece):
        return pltpu.make_async_remote_copy(
            src_ref=core_out.at[piece],
            dst_ref=core_in.at[piece],
            send_sem=sum_core_send.at[piece],
            recv_sem=sum_core_recv.at[piece],
            device_id={"rep": sibling},
            device_id_type=MESH,
        )

    def sum_head(piece, k):
        return pltpu.make_async_remote_copy(
            src_ref=head_out.at[piece, k - 1],
            dst_ref=head_in.at[piece, k - 1],
            send_sem=sum_head_send.at[piece, k - 1],
            recv_sem=sum_head_recv.at[piece, k - 1],
            device_id={"head": lax.rem(x + k, n_head)},
            device_id_type=MESH,
        )

    def project(piece):
        product = jnp.dot(
            expanded[...],
            out_proj[:, piece * columns : (piece + 1) * columns],
            preferred_element_type=jnp.float32,
        )
        partial[piece] = product.reshape(n_head * 2, out_rows, columns)
        for k in range(n_head):
            core_out[piece, k] = partial[
                piece, lax.rem(x + k, n_head) * 2 + sibling
            ].astype(jnp.bfloat16)
        sum_core(piece).start()

    def add_core(piece):
        sum_core(piece).wait_recv()
        for k in range(1, n_head):
            head_out[piece, k - 1] = (
                partial[piece, lax.rem(x + k, n_head) * 2 + c]
                + core_in[piece, k].astype(jnp.float32)
            ).astype(jnp.bfloat16)
            sum_head(piece, k).start()

    for piece in range(pieces):
        project(piece)
        if piece:
            add_core(piece - 1)
    add_core(pieces - 1)
    for piece in range(pieces):
        total = partial[piece, x * 2 + c] + core_in[piece, 0].astype(jnp.float32)
        for k in range(1, n_head):
            sum_head(piece, k).wait_recv()
            total = total + head_in[piece, k - 1].astype(jnp.float32)
        out_ref[:, piece * columns : (piece + 1) * columns] = total.astype(out_ref.dtype)

    own_copy(c).wait_send()
    for b in range(1, levels + 1):
        for i in range(per_share):

            @pl.when(seq_start(b, i))
            def _():
                for part in range(len(parts)):
                    seq_copy(b, i, part).wait_send()

            @pl.when(z >= 2 ** (b - 1))
            def _():
                for part in range(len(parts)):
                    for k in range(1, n_head):
                        head_copy(b, k, i, part).wait_send()
                    for k in range(n_head):
                        core_copy(b, k, i, c, part).wait_send()

    for piece in range(pieces):
        sum_core(piece).wait_send()
        for k in range(1, n_head):
            sum_head(piece, k).wait_send()


def shards(query_latent, query_rope, latent, key_rope, value_up, out_proj):
    q_dev, heads, width = query_latent.shape
    rope_width = key_rope.shape[0]
    half = latent.shape[0]
    n_seq, n_head = lax.axis_size("seq"), lax.axis_size("head")
    levels = min(4, n_seq // 4 + 1)
    chunk = lanes
    per_share = half // (n_head * chunk)
    chunks = half // chunk
    pack = rope_width * chunk // width
    rows = q_dev * heads
    features = out_proj.shape[1]
    columns = column_width(features, 8 * lanes)
    pieces = features // columns
    out_rows = q_dev // (2 * n_head)
    dims = (n_seq, n_head, levels, heads, q_dev, width, rope_width, chunk, per_share)
    if heads % 8:
        query_latent = query_latent.reshape(rows, width)
    bf16, f32 = jnp.bfloat16, jnp.float32
    dma = pltpu.SemaphoreType.DMA
    others = max(1, n_head - 1)
    return pl.pallas_call(
        functools.partial(kernel, dims),
        out_shape=jax.ShapeDtypeStruct((out_rows, features), bf16),
        in_specs=[pl.BlockSpec(memory_space=pl.ANY)] * 6,
        out_specs=pl.BlockSpec(memory_space=pltpu.VMEM),
        scratch_shapes=[
            pltpu.VMEM((levels + 1, 2, chunks, chunk + pack, width), bf16),
            pltpu.VMEM(query_latent.shape, bf16),
            pltpu.VMEM(query_rope.shape, bf16),
            pltpu.VMEM(key_rope.shape, bf16),
            pltpu.VMEM(value_up.shape, bf16),
            pltpu.VMEM(out_proj.shape, bf16),
            pltpu.VMEM((rows, width + rope_width), bf16),
            pltpu.VMEM((rows, lanes), f32),
            pltpu.VMEM((width + rope_width, 2 * half), bf16),
            pltpu.VMEM((rows, lanes), f32),
            pltpu.VMEM((rows, lanes), f32),
            pltpu.VMEM((width // lanes, rows, lanes), f32),
            pltpu.VMEM((q_dev, heads * value_up.shape[2]), bf16),
            pltpu.VMEM((pieces, 2 * n_head, out_rows, columns), f32),
            pltpu.VMEM((pieces, n_head, out_rows, columns), bf16),
            pltpu.VMEM((pieces, n_head, out_rows, columns), bf16),
            pltpu.VMEM((pieces, others, out_rows, columns), bf16),
            pltpu.VMEM((pieces, others, out_rows, columns), bf16),
            dma((chunks + 5,)),
            dma,
            dma,
            dma((levels, per_share, 2)),
            dma((levels, per_share, 2)),
            dma((levels, others, per_share, 2)),
            dma((levels, others, per_share, 2)),
            dma((levels, n_head, per_share, 2)),
            dma((levels, n_head, per_share, 2)),
            dma((pieces,)),
            dma((pieces,)),
            dma((pieces, others)),
            dma((pieces, others)),
        ],
        compiler_params=pltpu.CompilerParams(
            collective_id=0, has_side_effects=True, vmem_limit_bytes=63 * 1024 * 1024
        ),
        cost_estimate=pl.CostEstimate(
            flops=2 * rows * (levels + 1) * 2 * half * (2 * width + rope_width),
            bytes_accessed=2 * (rows * width + out_proj.size),
            transcendentals=rows * (levels + 1) * 2 * half,
        ),
    )(query_latent, query_rope, latent, key_rope, value_up, out_proj)


def solution(mesh):
    placed = (
        P(("grp", "seq"), ("head", "rep"), None),
        P(("grp", "seq"), ("head", "rep")),
        P(("grp", "seq", "rep"), None),
        P(None, ("grp", "seq", "rep")),
        P(("head", "rep"), None, None),
        P(("head", "rep"), None),
    )
    return jax.shard_map(
        shards,
        mesh=mesh,
        in_specs=placed,
        out_specs=P(("grp", "seq", "head", "rep"), None),
        check_vma=False,
    )
```
